256 devices in a mesh: tm: 64 (over x, y_hi, z), corpus: 4 (over y_lo, core).
Axes of the slice: x: 4, y: 4 (y_hi: 2, y_lo: 2; y = y_hi * 2 + y_lo), z: 8, core: 2. Of those that a mesh axis runs over, the one named last changes fastest.
Arguments:
- wave: float32 [4, 33554432], P('corpus', 'tm'), may hold values from -40 to 40, as said below
- dict_init: float32 [1025, 512], replicated, may hold values from 0.01 to 0.1
- act_init: float32 [4, 512, 32768], P('corpus', None, 'tm'), may hold values from 0.25 to 2.5
Outputs:
- dictionary: float32 [1025, 512], replicated
- activations: float32 [4, 512, 32768], P('corpus', None, 'tm')
The draws below stay inside these ranges and needn't reach their ends.
Inputs may be any that keep to these rules, and one draw needn't show every extreme that they name: `wave`: waveform samples.
All inputs are finite; a program needn't handle non-finite values.
Results may differ from the reference program's by a relative error of at most 0.00048.
Values sent between devices are 32-bit elements; how exact they have to be, the bound alone decides.
A program may use at most 64 MiB of HBM per device.

```python
import math
import jax
import jax.numpy as jnp
from jax import lax

WIN = 2048
HOP = 1024
BINS = 1025
K = 512
ITERS = 3
STREAMS = 4
FRAMES = 32768
SAMPLES = 33554432


def draw_wave(key, part):
    key = jax.random.fold_in(key, 7)
    key_noise = jax.random.fold_in(key, 0)
    key_loud = jax.random.fold_in(key, 1)
    key_bins = jax.random.fold_in(key, 3)
    key_color = jax.random.fold_in(key, 4)
    key_level = jax.random.fold_in(key, 5)
    reach = SAMPLES // 16
    position = jnp.arange(SAMPLES, dtype=jnp.float32) / SAMPLES
    ramp = jnp.exp(jnp.log(3.0) * position)[None, :]
    loud = jnp.exp(jax.random.uniform(key_loud, (STREAMS, FRAMES), jnp.float32, jnp.log(0.3), jnp.log(2.0)))
    loud = jnp.repeat(loud, HOP, axis=1)
    noise = jnp.clip(jax.random.normal(key_noise, (STREAMS, SAMPLES), jnp.float32), -4.0, 4.0)
    tone_bin = jax.random.randint(key_bins, (STREAMS, 16), 2, BINS - 1)
    tone_bin = jnp.repeat(tone_bin, reach, axis=1)
    sample_index = jnp.arange(SAMPLES, dtype=jnp.int32) % WIN
    phase_int = sample_index[None, :] * tone_bin % WIN
    level = jax.random.uniform(key_level, (STREAMS, 16), jnp.float32, 1.0, 2.0)
    level = jnp.repeat(level, reach, axis=1)
    tone = level * jnp.sin(phase_int.astype(jnp.float32) * (2.0 * jnp.pi / WIN))
    color = jax.random.uniform(key_color, (STREAMS, 16), jnp.float32, -0.85, 0.85)
    color = jnp.repeat(color, reach, axis=1)
    earlier = jnp.concatenate([jnp.zeros((STREAMS, 1), jnp.float32), noise[:, :-1]], 1)
    colored = 0.5 * (noise + color * earlier)
    return (colored + tone) * loud * ramp


def block_scale(rng, dims, shards, smallest, largest):
    gain, own = 1.0, jax.random.fold_in(rng, 6)
    for axis_at, shards_of in shards:
        heights = jnp.exp(jax.random.uniform(jax.random.fold_in(own, axis_at), (shards_of,), jnp.float32, smallest / len(shards), largest / len(shards)))
        gain = gain * jnp.repeat(heights, dims[axis_at] // shards_of).reshape([-1 if axis == axis_at else 1 for axis in range(len(dims))])
    return gain


def setup_inputs(seed: int = 0) -> dict:
    splits = jax.random.split(jax.random.key(seed), 4)
    return {
        "wave": draw_wave(jax.random.fold_in(splits[3], 71), 0),
        "dict_init": jnp.clip(jnp.exp(jax.random.uniform(splits[1], (BINS, K), jnp.float32, math.log(0.01), math.log(0.1))), 0.01, 0.1),
        "act_init": jnp.clip(jnp.exp(math.log(2.5) - 2.3025851 * jax.random.uniform(splits[2], (STREAMS, K, FRAMES), jnp.float32) ** block_scale(splits[2], (STREAMS, K, FRAMES), ((0, 4), (2, 64)), -0.2, 0.2)), 0.25, 2.5),
    }


HI = lax.Precision.HIGHEST

def make_table():
    index_n = jnp.arange(WIN, dtype=jnp.int32)[None, :]
    index_k = jnp.arange(BINS, dtype=jnp.int32)[:, None]
    phase = (index_k * index_n % WIN).astype(jnp.float32) * (2.0 * jnp.pi / WIN)
    return jnp.concatenate([jnp.cos(phase), jnp.sin(phase)], 0).astype(jnp.bfloat16)

def reference(wave, dict_init, act_init):
    index_n = jnp.arange(WIN, dtype=jnp.float32)
    window = 0.5 - 0.5 * jnp.cos(2.0 * jnp.pi * index_n / WIN)
    table = make_table()
    mags = []
    for s in range(STREAMS):
        rows = wave[s].reshape(FRAMES, HOP)
        ext = jnp.concatenate([rows, jnp.zeros((1, HOP), jnp.float32)], 0)
        frames = (jnp.concatenate([ext[:-1], ext[1:]], 1) * window[None, :]).astype(jnp.bfloat16)
        spec = lax.dot_general(table, frames, (((1,), (1,)), ((), ())), preferred_element_type=jnp.float32)
        mags.append(jnp.sqrt(spec[:BINS] ** 2 + spec[BINS:] ** 2 + 0.01))
    mag = jnp.stack(mags, 0)
    dictionary = dict_init
    activations = act_init
    for step in range(ITERS):
        approx = jnp.einsum('bk,skf->sbf', dictionary, activations, precision=HI)
        ratio = mag / approx
        colsum = lax.optimization_barrier(jnp.sum(dictionary, 0))
        activations = activations * jnp.einsum('bk,sbf->skf', dictionary, ratio, precision=HI) / colsum[None, :, None]
        approx = jnp.einsum('bk,skf->sbf', dictionary, activations, precision=HI)
        ratio = mag / approx
        numer = jnp.einsum('sbf,skf->bk', ratio, activations, precision=HI)
        hsum = lax.optimization_barrier(jnp.sum(activations, (0, 2)))
        dictionary = dictionary * numer / hsum[None, :]
    return (dictionary, activations)
```

```python
import functools

import jax
import jax.numpy as jnp
import numpy as np
from jax import lax
from jax.experimental import pallas as pl
from jax.experimental.pallas import tpu as pltpu
from jax.sharding import PartitionSpec as P

WIN = 2048
HOP = 1024
BINS = 1025
K = 512
ITERS = 3
MESH = pl.DeviceIdType.MESH
F32 = jnp.float32
BF16 = jnp.bfloat16


def shifted(value, axis, steps):
    count = lax.axis_size(axis)
    first, last = (max(0, -steps), min(count, count - steps))
    return lax.ppermute(value, axis, [(source, source + steps) for source in range(first, last)])


def make_table():
    index_n = np.arange(WIN, dtype=np.int64)[None, :]
    index_k = np.arange(BINS, dtype=np.int64)[:, None]
    phase = (index_k * index_n % WIN).astype(np.float64) * (2.0 * np.pi / WIN)
    table = np.concatenate([np.cos(phase), np.sin(phase)], 0).astype(np.float32)
    return table.astype(jnp.bfloat16)


def device(x, y, z, k):
    return (x * 16 + (y // 2) * 8 + z, (y % 2) * 2 + k)


CORE, CORE_E = 0, 2
P1, P2, P3 = 3, 11, 19
E1, E2, E3 = 35, 39, 43
G3, G2, G1, GC = 51, 67, 75, 83
SEMS = 91


def nmf_kernel(
    mag, d0, a0, d_out, a_out,
    dland, dbf, debf, drow, abf, atbf, upd, csum,
    cs, cr, es, er, own,
    r1, r2, r3, s2, s3, re1, re2, re3, esum, ssem, rsem,
):
    tm, corpus = lax.axis_index("tm"), lax.axis_index("corpus")
    x, z, k = tm // 16, tm % 8, corpus % 2
    y = ((tm // 8) % 2) * 2 + corpus // 2
    core = device(x, y, z, 1 - k)

    def at_x(i):
        return device(i, y, z, k)

    def at_y(i):
        return device(x, i, z, k)

    def at_z(i):
        return device(x, y, i, k)

    axes = (((x, at_x), (y, at_y)), ((y, at_y), (x, at_x)))

    barrier = pltpu.get_barrier_semaphore()
    pl.semaphore_signal(barrier, inc=1, device_id=core, device_id_type=MESH)
    for d in range(1, 4):
        pl.semaphore_signal(barrier, inc=1, device_id=at_x((x + d) % 4), device_id_type=MESH)
        pl.semaphore_signal(barrier, inc=1, device_id=at_y((y + d) % 4), device_id_type=MESH)
    for d in range(1, 8):
        pl.semaphore_signal(barrier, inc=1, device_id=at_z((z + d) % 8), device_id_type=MESH)
    pl.semaphore_wait(barrier, 14)

    def copy(src, dst, send, recv, to):
        return pltpu.make_async_remote_copy(
            src_ref=src, dst_ref=dst, send_sem=ssem.at[send], recv_sem=rsem.at[recv],
            device_id=to, device_id_type=MESH,
        )

    def rows(start, count):
        return pl.ds(pl.multiple_of(start, count), count)

    def dot(a, b):
        return jnp.dot(a, b, preferred_element_type=F32)

    def dot_t(a, b):
        return lax.dot_general(a, b, (((0,), (0,)), ((), ())), preferred_element_type=F32)

    ones = jnp.ones((256, 128), BF16)
    row_id = lax.broadcasted_iota(jnp.int32, (16, K), 0)

    def row_of(tile):
        return jnp.concatenate([tile[i : i + 1, :] for i in range(4)], 1)

    def ratio_e():
        approx = dot(debf[...], abf[...])
        ratio = mag[1024:1025, :] / approx[0:1, :]
        return jnp.where(row_id == 0, ratio, jnp.where(row_id == 8, 1.0, 0.0)).astype(BF16)

    def set_row(row):
        drow[...] = row
        debf[...] = jnp.where(row_id == 0, row, 0.0).astype(BF16)

    def ratio_at(at):
        approx = dot(dbf[rows(at, 256), :], abf[...])
        return (mag[rows(at, 256), :] / approx).astype(BF16)

    def first_half(at):
        ratio = ratio_at(at)
        part = dbf[rows(at, 256), :]
        upd[...] += dot_t(part, ratio)
        csum[...] += dot_t(part, ones)

    def start_first_half():
        ratio = ratio_e()
        upd[...] = dot_t(debf[...], ratio)
        csum[...] = dot_t(debf[...], ones[0:16])

    def set_act():
        value = a_out[...]
        abf[...] = value.astype(BF16)
        atbf[...] = value.T.astype(BF16)

    def finish_first_half():
        scale = 1.0 / csum[...]
        for i in range(4):
            cols = slice(i * 128, i * 128 + 128)
            a_out[:, cols] = a_out[:, cols] * upd[:, cols] * scale
        set_act()

    a_out[...] = a0[...]
    abf[...] = a0[...].astype(BF16)
    dland[...] = d0[0:1024, :]
    dbf[...] = d0[0:1024, :].astype(BF16)
    set_row(d0[1024:1025, :])
    start_first_half()

    @pl.loop(0, 4)
    def _(c):
        first_half(c * 256)

    finish_first_half()

    tile_row = (z // 4) * 8
    tile_col = pl.ds(pl.multiple_of((z % 4) * 128, 128), 128)
    near = (2, 1, 3)
    near_z = (4, 3, 5, 2, 6, 1, 7)

    @pl.loop(0, ITERS)
    def _(t):
        sends = []

        def send(*args):
            c = copy(*args)
            c.start()
            sends.append(c)

        def arrived(dst, recv):
            copy(dst, dst, 0, recv, core).wait_recv()

        ratio = ratio_e()
        line = dot(ratio, atbf[...])
        es[...] = jnp.concatenate(
            [line[r : r + 1, i * 128 : i * 128 + 128] for r in (0, 8) for i in range(4)], 0
        )
        send(es, er, CORE_E, CORE_E, core)
        for p in range(2):
            part = slice(p * 256, p * 256 + 256)
            cs[part, :] = dot(ratio_at((1 - k) * 512 + p * 256), atbf[...])
            send(cs.at[part, :], cr.at[part, :], CORE + p, CORE + p, core)

        def exchange_e(base, dst, me, at, count, order):
            for d in order:
                to = (me + d) % count
                send(dst.at[me], dst.at[me], base + d, base + me, at(to))

        for p in range(2):
            me, at = axes[p][0]
            part = slice(p * 256, p * 256 + 256)
            value = dot(ratio_at(k * 512 + p * 256), atbf[...])
            arrived(cr.at[part, :], CORE + p)
            own[part, :] = value + cr[part, :]
            for d in near:
                to = (me + d) % 4
                send(
                    own.at[rows(p * 256 + to * 64, 64), :], r1.at[p, me],
                    P1 + p * 4 + d, P1 + p * 4 + me, at(to),
                )
            if p == 0:
                arrived(er, CORE_E)
                re1[x] = es[...] + er[...]
                exchange_e(E1, re1, x, at_x, 4, near)
            r1[p, me] = own[rows(p * 256 + me * 64, 64), :]

        for p in range(2):
            before = axes[p][0][0]
            me, at = axes[p][1]
            for d in (1, 3, 2):
                i = (before + d) % 4
                arrived(r1.at[p, i], P1 + p * 4 + i)
            s2[p] = (r1[p, 0] + r1[p, 1]) + (r1[p, 2] + r1[p, 3])
            for d in near:
                to = (me + d) % 4
                send(s2.at[p, rows(to * 16, 16), :], r2.at[p, me], P2 + p * 4 + d, P2 + p * 4 + me, at(to))
            if p == 0:
                for d in (1, 3, 2):
                    i = (x + d) % 4
                    arrived(re1.at[i], E1 + i)
                re2[y] = (re1[0] + re1[1]) + (re1[2] + re1[3])
                exchange_e(E2, re2, y, at_y, 4, near)
            r2[p, me] = s2[p, rows(me * 16, 16), :]

        for p in range(2):
            before = axes[p][1][0]
            for d in (1, 3, 2):
                i = (before + d) % 4
                arrived(r2.at[p, i], P2 + p * 4 + i)
            total = (r2[p, 0] + r2[p, 1]) + (r2[p, 2] + r2[p, 3])
            for i in range(8):
                s3[p, i] = total[(i // 4) * 8 : (i // 4) * 8 + 8, (i % 4) * 128 : (i % 4) * 128 + 128]
            for d in near_z:
                to = (z + d) % 8
                send(s3.at[p, to], r3.at[p, z], P3 + p * 8 + d, P3 + p * 8 + z, at_z(to))
            if p == 0:
                for d in (1, 3, 2):
                    i = (y + d) % 4
                    arrived(re2.at[i], E2 + i)
                re3[z] = (re2[0] + re2[1]) + (re2[2] + re2[3])
                exchange_e(E3, re3, z, at_z, 8, near_z)
            r3[p, z] = s3[p, z]

        base = [k * 512 + p * 256 + axes[p][0][0] * 64 for p in range(2)]
        small = [base[p] + axes[p][1][0] * 16 for p in range(2)]
        for p in range(2):
            for d in (1, 7, 2, 6, 3, 5, 4):
                i = (z + d) % 8
                arrived(r3.at[p, i], P3 + p * 8 + i)
            if p == 0:
                for d in (1, 7, 2, 6, 3, 5, 4):
                    i = (z + d) % 8
                    arrived(re3.at[i], E3 + i)
                esum[...] = ((re3[0] + re3[1]) + (re3[2] + re3[3])) + ((re3[4] + re3[5]) + (re3[6] + re3[7]))
            total = ((r3[p, 0] + r3[p, 1]) + (r3[p, 2] + r3[p, 3])) + ((r3[p, 4] + r3[p, 5]) + (r3[p, 6] + r3[p, 7]))
            tile = (rows(small[p] + tile_row, 8), tile_col)
            dland[tile] = dland[tile] * total / esum[pl.ds(4 + z % 4, 1), :]
            for d in near_z:
                to = (z + d) % 8
                send(dland.at[tile], dland.at[tile], G3 + p * 8 + d, G3 + p * 8 + z, at_z(to))

        esum_v = esum[...]
        set_row(drow[...] * row_of(esum_v[0:4, :]) / row_of(esum_v[4:8, :]))

        for p in range(2):
            me, at = axes[p][1]
            for d in (1, 7, 2, 6, 3, 5, 4):
                i = (z + d) % 8
                tile = (
                    rows(small[p] + (i // 4) * 8, 8),
                    pl.ds(pl.multiple_of((i % 4) * 128, 128), 128),
                )
                arrived(dland.at[tile], G3 + p * 8 + i)
            piece = dland.at[rows(small[p], 16), :]
            for d in near:
                to = (me + d) % 4
                send(piece, piece, G2 + p * 4 + d, G2 + p * 4 + me, at(to))

        for p in range(2):
            me, at = axes[p][0]
            second = axes[p][1][0]
            for d in (1, 3, 2):
                i = (second + d) % 4
                arrived(dland.at[rows(base[p] + i * 16, 16), :], G2 + p * 4 + i)
            piece = dland.at[rows(base[p], 64), :]
            for d in near:
                to = (me + d) % 4
                send(piece, piece, G1 + p * 4 + d, G1 + p * 4 + me, at(to))
            send(piece, piece, GC + p * 4, GC + p * 4 + me, core)

        for d in (1, 3, 2):
            for p in range(2):
                i = (axes[p][0][0] + d) % 4
                piece = dland.at[rows(k * 512 + p * 256 + i * 64, 64), :]
                arrived(piece, G1 + p * 4 + i)
                send(piece, piece, GC + p * 4 + d, GC + p * 4 + i, core)

        def consume(at):
            @pl.when(t < ITERS - 1)
            def _():
                dbf[rows(at, 256), :] = dland[rows(at, 256), :].astype(BF16)
                first_half(at)

        @pl.when(t < ITERS - 1)
        def _():
            start_first_half()

        for p in range(2):
            consume(k * 512 + p * 256)
        for p in range(2):
            for i in range(4):
                arrived(dland.at[rows((1 - k) * 512 + p * 256 + i * 64, 64), :], GC + p * 4 + i)
            consume((1 - k) * 512 + p * 256)

        @pl.when(t < ITERS - 1)
        def _():
            finish_first_half()

        for c in sends:
            c.wait_send()

    d_out[0:1024, :] = dland[...]
    d_out[1024:1025, :] = drow[...]


def nmf(mag, dictionary, activations):
    vmem = pl.BlockSpec(memory_space=pltpu.VMEM)
    return pl.pallas_call(
        nmf_kernel,
        out_shape=[
            jax.ShapeDtypeStruct((BINS, K), F32),
            jax.ShapeDtypeStruct((K, 512), F32),
        ],
        in_specs=[vmem] * 3,
        out_specs=[vmem] * 2,
        scratch_shapes=[
            pltpu.VMEM((1024, K), F32),
            pltpu.VMEM((1024, K), BF16),
            pltpu.VMEM((16, K), BF16),
            pltpu.VMEM((1, K), F32),
            pltpu.VMEM((K, 512), BF16),
            pltpu.VMEM((512, K), BF16),
            pltpu.VMEM((K, 512), F32),
            pltpu.VMEM((K, 128), F32),
            pltpu.VMEM((512, K), F32),
            pltpu.VMEM((512, K), F32),
            pltpu.VMEM((8, 128), F32),
            pltpu.VMEM((8, 128), F32),
            pltpu.VMEM((512, K), F32),
            pltpu.VMEM((2, 4, 64, K), F32),
            pltpu.VMEM((2, 4, 16, K), F32),
            pltpu.VMEM((2, 8, 8, 128), F32),
            pltpu.VMEM((2, 64, K), F32),
            pltpu.VMEM((2, 8, 8, 128), F32),
            pltpu.VMEM((4, 8, 128), F32),
            pltpu.VMEM((4, 8, 128), F32),
            pltpu.VMEM((8, 8, 128), F32),
            pltpu.VMEM((8, 128), F32),
            pltpu.SemaphoreType.DMA((SEMS,)),
            pltpu.SemaphoreType.DMA((SEMS,)),
        ],
        compiler_params=pltpu.CompilerParams(
            collective_id=0, has_side_effects=True, vmem_limit_bytes=48 * 2**20
        ),
        name="nmf",
    )(mag, dictionary, activations)


def per_device(wave, dict_init, act_init):
    rows = wave[0].reshape(-1, HOP)
    follow = shifted(rows[0:1], "tm", -1)
    index_n = np.arange(WIN, dtype=np.float64)
    window = jnp.asarray((0.5 - 0.5 * np.cos(2.0 * np.pi * index_n / WIN)).astype(np.float32))
    ext = jnp.concatenate([rows, follow], 0)
    frames = (jnp.concatenate([ext[:-1], ext[1:]], 1) * window[None, :]).astype(BF16)
    spec = lax.dot_general(
        jnp.asarray(make_table()), frames, (((1,), (1,)), ((), ())), preferred_element_type=F32
    )
    mag = jnp.sqrt(spec[:BINS] ** 2 + spec[BINS:] ** 2 + 0.01)
    dictionary, activations = nmf(mag, dict_init, act_init[0])
    return (dictionary, activations[None])


def solution(mesh):
    in_specs = (P("corpus", "tm"), P(), P("corpus", None, "tm"))
    out_specs = (P(), P("corpus", None, "tm"))
    return jax.shard_map(
        per_device, mesh=mesh, in_specs=in_specs, out_specs=out_specs, check_vma=False
    )
```

```python
import functools

import jax
import jax.numpy as jnp
import numpy as np
from jax import lax
from jax.experimental import pallas as pl
from jax.experimental.pallas import tpu as pltpu
from jax.sharding import PartitionSpec as P

WIN = 2048
HOP = 1024
BINS = 1025
K = 512
ITERS = 3
MESH = pl.DeviceIdType.MESH
F32 = jnp.float32
BF16 = jnp.bfloat16


def make_table():
    index_n = np.arange(WIN, dtype=np.int64)[None, :]
    index_k = np.arange(BINS, dtype=np.int64)[:, None]
    phase = (index_k * index_n % WIN).astype(np.float64) * (2.0 * np.pi / WIN)
    last = np.zeros((16, WIN))
    last[0], last[8] = np.cos(phase[BINS - 1]), np.sin(phase[BINS - 1])
    table = np.concatenate([np.cos(phase[: BINS - 1]), np.sin(phase[: BINS - 1]), last], 0)
    return table.astype(np.float32).astype(jnp.bfloat16)


def make_window():
    index_n = np.arange(WIN, dtype=np.float64)
    return (0.5 - 0.5 * np.cos(2.0 * np.pi * index_n / WIN)).astype(np.float32).reshape(16, 128)


def device(x, y, z, k):
    return (x * 16 + (y // 2) * 8 + z, (y % 2) * 2 + k)


CORE, CORE_E = 0, 4
P1, P2, P3 = 5, 13, 15
E1, E2, E3 = 17, 18, 19
G3, G2, G1, GC = 20, 22, 30, 38
SEMS = 46


def atom_scale(index):
    value = index * 0.6180339887
    return 1.0 + (value - jnp.floor(value))


def nmf_kernel(
    wave, table, window, d0, a0, d_out, a_out,
    samples, frames, halo, tail, tab, spec, mag,
    dland, dbf, debf, drow, abf, atbf, upd, csum,
    cs, cr, es, er, own,
    r1, r2, r3, s2, s3, re1, re2, re3, esum, ssem, rsem, lsem, hsem,
):
    tm, corpus = lax.axis_index("tm"), lax.axis_index("corpus")
    x, z, k = tm // 16, tm % 8, corpus % 2
    y = ((tm // 8) % 2) * 2 + corpus // 2
    core = device(x, y, z, 1 - k)

    def at_x(i):
        return device(i, y, z, k)

    def at_y(i):
        return device(x, i, z, k)

    def at_z(i):
        return device(x, y, i, k)

    axes = (((x, at_x), (y, at_y)), ((y, at_y), (x, at_x)))

    loads = [
        pltpu.make_async_copy(wave, samples.at[0:4096, :], lsem.at[0]),
        pltpu.make_async_copy(d0.at[0:1024, :], dland, lsem.at[1]),
        pltpu.make_async_copy(a0, a_out, lsem.at[2]),
    ]
    for c in range(4):
        for h in range(2):
            part = slice(h * 1024 + c * 256, h * 1024 + c * 256 + 256)
            loads.append(pltpu.make_async_copy(table.at[part, :], tab.at[part, :], lsem.at[3 + 2 * c + h]))
    loads.append(pltpu.make_async_copy(table.at[2048:2064, :], tab.at[2048:2064, :], lsem.at[11]))
    loads.append(pltpu.make_async_copy(d0.at[1024:1025, :], drow, lsem.at[12]))
    for i in (0, 3, 4, 11, 5, 6, 7, 8, 9, 10, 2, 1, 12):
        loads[i].start()

    barrier = pltpu.get_barrier_semaphore()
    before, after = ((tm + 63) % 64, corpus), ((tm + 1) % 64, corpus)
    for neighbour in (before, after):
        pl.semaphore_signal(barrier, inc=1, device_id=neighbour, device_id_type=MESH)
    pl.semaphore_signal(barrier, inc=1, device_id=core, device_id_type=MESH)
    for d in range(1, 4):
        pl.semaphore_signal(barrier, inc=1, device_id=at_x((x + d) % 4), device_id_type=MESH)
        pl.semaphore_signal(barrier, inc=1, device_id=at_y((y + d) % 4), device_id_type=MESH)
    for d in range(1, 8):
        pl.semaphore_signal(barrier, inc=1, device_id=at_z((z + d) % 8), device_id_type=MESH)

    def copy(src, dst, send, recv, to):
        return pltpu.make_async_remote_copy(
            src_ref=src, dst_ref=dst, send_sem=ssem.at[send], recv_sem=rsem.at[recv],
            device_id=to, device_id_type=MESH,
        )

    def rows(start, count, step=None):
        return pl.ds(pl.multiple_of(start, step or count), count)

    def dot(a, b):
        return jnp.dot(a, b, preferred_element_type=F32)

    def dot_t(a, b):
        return lax.dot_general(a, b, (((0,), (0,)), ((), ())), preferred_element_type=F32)

    def dot_nt(a, b):
        return lax.dot_general(a, b, (((1,), (1,)), ((), ())), preferred_element_type=F32)

    def split(value):
        high = value.astype(BF16)
        return high, (value - high.astype(F32)).astype(BF16)

    row_id = lax.broadcasted_iota(jnp.int32, (16, K), 0)

    def row_of(tile):
        return jnp.concatenate([tile[i : i + 1, :] for i in range(4)], 1)

    def ratio_e():
        approx = dot(debf[0:16, :], abf[...])
        return mag[1024:1025, :] / approx[0:1, :]

    def set_row(row):
        drow[...] = row
        high, low = split(jnp.where(row_id == 0, row, 0.0))
        debf[0:16, :] = high
        debf[16:32, :] = low

    def products(high, low, ratio):
        rh, rl = split(ratio)
        left = jnp.concatenate([high, high, low], 0)
        update = dot_t(left, jnp.concatenate([rh, rl, rh], 0))
        count = high.shape[0]
        return update, dot_t(left[count:], jnp.ones((2 * count, 128), BF16))

    def first_half(high, low, target):
        ratio = target / dot(high, abf[...])
        update, total = products(high, low, ratio)
        upd[...] += update
        csum[...] += total

    def start_first_half():
        ratio = jnp.where(row_id == 0, ratio_e(), 0.0)
        update, total = products(debf[0:16, :], debf[16:32, :], ratio)
        upd[...] = update
        csum[...] = total

    def set_act():
        value = a_out[...]
        abf[...] = value.astype(BF16)
        atbf[...] = value.T.astype(BF16)

    def finish_first_half():
        scale = 1.0 / csum[...]
        for i in range(4):
            cols = slice(i * 128, i * 128 + 128)
            a_out[:, cols] = a_out[:, cols] * upd[:, cols] * scale
        set_act()

    loads[0].wait()
    for c in range(8):
        cols = slice(c * 128, c * 128 + 128)
        frames[:, cols] = (samples[pl.ds(c, 512, stride=8), :] * window[c : c + 1, :]).astype(BF16)
    samples[4096:4104, :] = jnp.zeros((8, 128), F32)
    for c in range(8):
        cols = slice(1024 + c * 128, 1024 + c * 128 + 128)
        frames[:, cols] = (samples[pl.ds(8 + c, 512, stride=8), :] * window[8 + c : 9 + c, :]).astype(BF16)

    for c in range(4):
        if c == 1:
            pl.semaphore_wait(barrier, 16)
            greet = pltpu.make_async_remote_copy(
                src_ref=samples.at[0:8, :], dst_ref=halo, send_sem=hsem.at[0], recv_sem=hsem.at[1],
                device_id=before, device_id_type=MESH,
            )
            greet.start()
        for h in range(2):
            part = slice(h * 1024 + c * 256, h * 1024 + c * 256 + 256)
            loads[3 + 2 * c + h].wait()
            spec[part, :] = dot_nt(tab[part, :], frames[...])
    loads[11].wait()
    spec[2048:2064, :] = dot_nt(tab[2048:2064, :], frames[...])

    loads[1].wait()
    loads[2].wait()
    loads[12].wait()
    atom_row = lax.broadcasted_iota(jnp.int32, (8, K), 1).astype(F32)[0:1]
    atom_col = lax.broadcasted_iota(jnp.int32, (K, 128), 0).astype(F32)
    inverse = 1.0 / atom_scale(atom_row)
    scale = atom_scale(atom_col)
    for i in range(4):
        cols = slice(i * 128, i * 128 + 128)
        value = a_out[:, cols] * scale
        a_out[:, cols] = value
        abf[:, cols] = value.astype(BF16)

    set_row(drow[...] * inverse)

    greet.wait()
    keep = jnp.where(tm == 63, 0.0, 1.0)
    tail[...] = jnp.zeros((128, 1024), BF16)
    last = halo[...] * window[8:16, :] * keep
    last = jnp.concatenate([last[c : c + 1, :] for c in range(8)], 1)
    row_16 = lax.broadcasted_iota(jnp.int32, (16, 1024), 0)
    tail[112:128, :] = jnp.where(row_16 == 15, last, 0.0).astype(BF16)
    spec[:, 384:512] += dot_nt(tab[:, 1024:2048], tail[...])

    real, imag = spec[2048:2049, :], spec[2056:2057, :]
    mag[1024:1025, :] = jnp.sqrt(real * real + imag * imag + 0.01)
    start_first_half()

    @pl.loop(0, 4)
    def _(c):
        real, imag = spec[rows(c * 256, 256), :], spec[rows(1024 + c * 256, 256), :]
        target = jnp.sqrt(real * real + imag * imag + 0.01)
        mag[rows(c * 256, 256), :] = target
        value = dland[rows(c * 256, 256), :] * inverse
        dland[rows(c * 256, 256), :] = value
        high, low = split(value)
        dbf[rows(c * 256, 256), :] = high
        first_half(high, low, target)

    finish_first_half()

    tile_row = (z // 4) * 8
    tile_col = pl.ds(pl.multiple_of((z % 4) * 128, 128), 128)
    near = (2, 1, 3)
    near_z = (4, 3, 5, 2, 6, 1, 7)

    @pl.loop(0, ITERS)
    def _(t):
        def send(*args):
            copy(*args).start()

        def arrived(dst, recv):
            copy(dst, dst, 0, recv, core).wait_recv()

        def left(src, sent):
            copy(src, src, sent, 0, core).wait_send()

        def group(half, jd):
            return [
                half * 512 + p * 256 + i * 64 + ((axes[p][1][0] + jd) % 4) * 16
                for p in range(2)
                for i in range(4)
            ]

        def gather(ref, starts):
            return jnp.concatenate([ref[rows(start, 16), :] for start in starts], 0)

        def numerator(half, jd):
            starts = group(half, jd)
            ratio = gather(mag, starts) / dot(gather(dbf, starts), abf[...])
            return dot(ratio.astype(BF16), atbf[...])

        def exchange_e(sem, dst, me, at, count, order):
            for d in order:
                send(dst.at[me], dst.at[me], sem, sem, at((me + d) % count))

        ratio = jnp.where(row_id == 0, ratio_e(), jnp.where(row_id == 8, 1.0, 0.0)).astype(BF16)
        line = dot(ratio, atbf[...])
        es[...] = jnp.concatenate(
            [line[r : r + 1, i * 128 : i * 128 + 128] for r in (0, 8) for i in range(4)], 0
        )
        send(es, er, CORE_E, CORE_E, core)

        def to_core(jd):
            cs[jd] = numerator(1 - k, jd)
            send(cs.at[jd], cr.at[jd], CORE + jd, CORE + jd, core)

        def to_first(jd):
            value = numerator(k, jd)
            arrived(cr.at[jd], CORE + jd)
            own[jd] = value + cr[jd]
            for d in near:
                for p in range(2):
                    (me, at), (other, _) = axes[p]
                    to, j = (me + d) % 4, (other + jd) % 4
                    send(
                        own.at[jd, rows(p * 64 + to * 16, 16), :], r1.at[p, me, rows(j * 16, 16), :],
                        P1 + p, P1 + p * 4 + j, at(to),
                    )
            for p in range(2):
                (me, _), (other, _) = axes[p]
                j = (other + jd) % 4
                r1[p, me, rows(j * 16, 16), :] = own[jd, rows(p * 64 + me * 16, 16), :]

        to_core(2)
        arrived(er, CORE_E)
        re1[x] = es[...] + er[...]
        exchange_e(E1, re1, x, at_x, 4, near)
        to_core(1)
        to_first(2)
        to_core(3)
        to_first(1)
        to_core(0)
        to_first(3)
        to_first(0)

        for jd in (2, 1, 3, 0):
            if jd == 1:
                arrived(re1.at[0:3], E1)
                re2[y] = (re1[0] + re1[1]) + (re1[2] + re1[3])
                exchange_e(E2, re2, y, at_y, 4, near)
            for p in range(2):
                me, at = axes[p][1]
                j = (me + jd) % 4
                arrived(r1.at[p, 0:3, 0:16, :], P1 + p * 4 + j)
                at_j = rows(j * 16, 16)
                total = (r1[p, 0, at_j, :] + r1[p, 1, at_j, :]) + (r1[p, 2, at_j, :] + r1[p, 3, at_j, :])
                if jd:
                    s2[p, jd] = total
                    send(s2.at[p, jd], r2.at[p, me], P2 + p, P2 + p, at(j))
                else:
                    r2[p, me] = total
        arrived(re2.at[0:3], E2)
        re3[z] = (re2[0] + re2[1]) + (re2[2] + re2[3])
        exchange_e(E3, re3, z, at_z, 8, near_z)

        for p in range(2):
            arrived(r2.at[p, 0:3], P2 + p)
            total = (r2[p, 0] + r2[p, 1]) + (r2[p, 2] + r2[p, 3])
            for i in range(8):
                s3[p, i] = total[(i // 4) * 8 : (i // 4) * 8 + 8, (i % 4) * 128 : (i % 4) * 128 + 128]
            for d in near_z:
                to = (z + d) % 8
                send(s3.at[p, to], r3.at[p, z], P3 + p, P3 + p, at_z(to))
            r3[p, z] = s3[p, z]

        base = [k * 512 + p * 256 + axes[p][0][0] * 64 for p in range(2)]
        small = [base[p] + axes[p][1][0] * 16 for p in range(2)]
        for p in range(2):
            arrived(r3.at[p, 0:7], P3 + p)
            total = ((r3[p, 0] + r3[p, 1]) + (r3[p, 2] + r3[p, 3])) + ((r3[p, 4] + r3[p, 5]) + (r3[p, 6] + r3[p, 7]))
            if p == 0:
                arrived(re3.at[0:7], E3)
                esum[...] = ((re3[0] + re3[1]) + (re3[2] + re3[3])) + ((re3[4] + re3[5]) + (re3[6] + re3[7]))
            tile = (rows(small[p] + tile_row, 8), tile_col)
            dland[tile] = dland[tile] * total / esum[pl.ds(4 + z % 4, 1), :]
            for d in near_z:
                send(dland.at[tile], dland.at[tile], G3 + p, G3 + p, at_z((z + d) % 8))

        esum_v = esum[...]
        set_row(drow[...] * row_of(esum_v[0:4, :]) / row_of(esum_v[4:8, :]))

        def spread(p, jd):
            (me, at), (other, _) = axes[p]
            j = (other + jd) % 4
            piece = dland.at[rows(base[p] + j * 16, 16), :]
            for d in near:
                send(piece, piece, G1 + p, G1 + p * 4 + j, at((me + d) % 4))
            send(piece, piece, GC + p, GC + p * 4 + j, core)

        for p in range(2):
            me, at = axes[p][1]
            piece = dland.at[rows(small[p], 16), :]
            arrived(dland.at[0:56, 0:128], G3 + p)
            for d in near:
                send(piece, piece, G2 + p, G2 + p * 4 + me, at((me + d) % 4))
        for p in range(2):
            spread(p, 0)

        for jd in (1, 3, 2):
            for p in range(2):
                j = (axes[p][1][0] + jd) % 4
                arrived(dland.at[rows(base[p] + j * 16, 16), :], G2 + p * 4 + j)
                spread(p, jd)

        def consume(half, jd):
            @pl.when(t < ITERS - 1)
            def _():
                starts = group(half, jd)
                high, low = split(gather(dland, starts))
                for n, start in enumerate(starts):
                    dbf[rows(start, 16), :] = high[n * 16 : n * 16 + 16, :]
                first_half(high, low, gather(mag, starts))

        def from_core(jd):
            for p in range(2):
                j = (axes[p][1][0] + jd) % 4
                arrived(dland.at[0:64, :], GC + p * 4 + j)
            consume(1 - k, jd)

        @pl.when(t < ITERS - 1)
        def _():
            start_first_half()

        past = None
        for jd in (0, 1, 3, 2):
            for p in range(2):
                (me, _), (other, _) = axes[p]
                j = (other + jd) % 4
                arrived(dland.at[0:48, :], G1 + p * 4 + j)
                for d in (1, 3, 2):
                    i = (me + d) % 4
                    piece = dland.at[rows(k * 512 + p * 256 + i * 64 + j * 16, 16), :]
                    send(piece, piece, GC + p, GC + p * 4 + j, core)
            consume(k, jd)
            if past is not None:
                from_core(past)
            past = jd
        from_core(past)

        @pl.when(t < ITERS - 1)
        def _():
            finish_first_half()

        left(es, CORE_E)
        for jd in range(4):
            left(cs.at[jd], CORE + jd)
        for p in range(2):
            left(dland.at[0:192, :], P1 + p)
            left(dland.at[0:48, :], P2 + p)
            left(s3.at[p, 0:7], P3 + p)
            left(s3.at[p, 0:7], G3 + p)
            left(dland.at[0:48, :], G2 + p)
            left(dland.at[0:192, :], G1 + p)
            left(dland.at[0:256, :], GC + p)
        left(re1.at[0:3], E1)
        left(re2.at[0:3], E2)
        left(re3.at[0:7], E3)

    d_out[0:1024, :] = dland[...]
    d_out[1024:1025, :] = drow[...]


def nmf(wave, dictionary, activations):
    vmem = pl.BlockSpec(memory_space=pltpu.VMEM)
    hbm = pl.BlockSpec(memory_space=pltpu.HBM)
    return pl.pallas_call(
        nmf_kernel,
        out_shape=[
            jax.ShapeDtypeStruct((BINS, K), F32),
            jax.ShapeDtypeStruct((K, 512), F32),
        ],
        in_specs=[hbm, hbm, vmem, hbm, hbm],
        out_specs=[vmem] * 2,
        scratch_shapes=[
            pltpu.VMEM((4104, 128), F32),
            pltpu.VMEM((512, WIN), BF16),
            pltpu.VMEM((8, 128), F32),
            pltpu.VMEM((128, HOP), BF16),
            pltpu.VMEM((2064, WIN), BF16),
            pltpu.VMEM((2064, 512), F32),
            pltpu.VMEM((1025, 512), F32),
            pltpu.VMEM((1024, K), F32),
            pltpu.VMEM((1024, K), BF16),
            pltpu.VMEM((32, K), BF16),
            pltpu.VMEM((1, K), F32),
            pltpu.VMEM((K, 512), BF16),
            pltpu.VMEM((512, K), BF16),
            pltpu.VMEM((K, 512), F32),
            pltpu.VMEM((K, 128), F32),
            pltpu.VMEM((4, 128, K), F32),
            pltpu.VMEM((4, 128, K), F32),
            pltpu.VMEM((8, 128), F32),
            pltpu.VMEM((8, 128), F32),
            pltpu.VMEM((4, 128, K), F32),
            pltpu.VMEM((2, 4, 64, K), F32),
            pltpu.VMEM((2, 4, 16, K), F32),
            pltpu.VMEM((2, 8, 8, 128), F32),
            pltpu.VMEM((2, 4, 16, K), F32),
            pltpu.VMEM((2, 8, 8, 128), F32),
            pltpu.VMEM((4, 8, 128), F32),
            pltpu.VMEM((4, 8, 128), F32),
            pltpu.VMEM((8, 8, 128), F32),
            pltpu.VMEM((8, 128), F32),
            pltpu.SemaphoreType.DMA((SEMS,)),
            pltpu.SemaphoreType.DMA((SEMS,)),
            pltpu.SemaphoreType.DMA((13,)),
            pltpu.SemaphoreType.DMA((2,)),
        ],
        compiler_params=pltpu.CompilerParams(
            collective_id=0, has_side_effects=True, vmem_limit_bytes=58 * 2**20
        ),
        name="nmf",
    )(wave, jnp.asarray(make_table()), jnp.asarray(make_window()), dictionary, activations)


def per_device(wave, dict_init, act_init):
    dictionary, activations = nmf(wave.reshape(-1, 128), dict_init, act_init[0])
    scale = atom_scale(jnp.arange(K, dtype=F32))
    return (dictionary * scale[None, :], (activations * (1.0 / scale)[:, None])[None])


def solution(mesh):
    in_specs = (P("corpus", "tm"), P(), P("corpus", None, "tm"))
    out_specs = (P(), P("corpus", None, "tm"))
    return jax.shard_map(
        per_device, mesh=mesh, in_specs=in_specs, out_specs=out_specs, check_vma=False
    )
```

```python
import functools

import jax
import jax.numpy as jnp
import numpy as np
from jax import lax
from jax.experimental import pallas as pl
from jax.experimental.pallas import tpu as pltpu
from jax.sharding import PartitionSpec as P

WIN = 2048
HOP = 1024
BINS = 1025
K = 512
ITERS = 3
MESH = pl.DeviceIdType.MESH
F32 = jnp.float32
BF16 = jnp.bfloat16


def make_table():
    index_n = np.arange(WIN, dtype=np.int64)[None, :]
    index_k = np.arange(BINS, dtype=np.int64)[:, None]
    phase = (index_k * index_n % WIN).astype(np.float64) * (2.0 * np.pi / WIN)
    last = np.zeros((16, WIN))
    last[0], last[8] = np.cos(phase[BINS - 1]), np.sin(phase[BINS - 1])
    table = np.concatenate([np.cos(phase[: BINS - 1]), np.sin(phase[: BINS - 1]), last], 0)
    return table.astype(np.float32).astype(jnp.bfloat16)


def make_window():
    index_n = np.arange(WIN, dtype=np.float64)
    return (0.5 - 0.5 * np.cos(2.0 * np.pi * index_n / WIN)).astype(np.float32).reshape(16, 128)


def device(x, y, z, k):
    return (x * 16 + (y // 2) * 8 + z, (y % 2) * 2 + k)


CORE, CORE_E, E1, E2, E3, P3 = 0, 4, 5, 6, 7, 8
P1, P2, G3, G2, G1, GC = 10, 26, 42, 58, 74, 90
SEMS = 106


def atom_scale(index):
    value = index * 0.6180339887
    return 1.0 + (value - jnp.floor(value))


def nmf_kernel(
    wave, table, window, d0, a0, d_result, a_result,
    a_out,    samples, frames, halo, tail, tab, spec, mag,
    dland, debf, drow, abf, atbf, upd, csum,
    cs, cr, es, er, own,
    r1, r2, r3, s2, s3, re1, re2, re3, esum, ssem, rsem, lsem, hsem,
):
    tm, corpus = lax.axis_index("tm"), lax.axis_index("corpus")
    x, z, k = tm // 16, tm % 8, corpus % 2
    y = ((tm // 8) % 2) * 2 + corpus // 2
    core = device(x, y, z, 1 - k)

    def at_x(i):
        return device(i, y, z, k)

    def at_y(i):
        return device(x, i, z, k)

    def at_z(i):
        return device(x, y, i, k)

    axes = (((x, at_x), (y, at_y)), ((y, at_y), (x, at_x)))

    loads = [
        pltpu.make_async_copy(d0.at[0:1024, :], dland, lsem.at[0]),
        pltpu.make_async_copy(a0, a_out, lsem.at[1]),
        pltpu.make_async_copy(d0.at[1024:1025, :], drow, lsem.at[2]),
        pltpu.make_async_copy(table.at[2048:2064, :], tab.at[2048:2064, :], lsem.at[3]),
    ]
    for c in range(4):
        part = slice(c * 512, c * 512 + 512)
        loads.append(pltpu.make_async_copy(table.at[part, :], tab.at[part, :], lsem.at[4 + c]))
    for c in range(4):
        part = slice(c * 1024, c * 1024 + 1024)
        loads.append(pltpu.make_async_copy(wave.at[part, :], samples.at[part, :], lsem.at[8 + c]))
    for i in (8, 9, 10, 11, 4):
        loads[i].start()

    def store(first):
        part = pl.ds(pl.multiple_of(first, 512), 512)
        return dland.at[part, :], d_result.at[part, :]

    stores = [
        pltpu.make_async_copy(a_out, a_result, lsem.at[12]),
        pltpu.make_async_copy(*store(k * 512), lsem.at[13]),
        pltpu.make_async_copy(*store((1 - k) * 512), lsem.at[14]),
        pltpu.make_async_copy(drow, d_result.at[1024:1025, :], lsem.at[15]),
    ]

    barrier = pltpu.get_barrier_semaphore()
    before, after = ((tm + 63) % 64, corpus), ((tm + 1) % 64, corpus)
    for neighbour in (before, after):
        pl.semaphore_signal(barrier, inc=1, device_id=neighbour, device_id_type=MESH)
    pl.semaphore_signal(barrier, inc=1, device_id=core, device_id_type=MESH)
    for d in range(1, 4):
        pl.semaphore_signal(barrier, inc=1, device_id=at_x((x + d) % 4), device_id_type=MESH)
        pl.semaphore_signal(barrier, inc=1, device_id=at_y((y + d) % 4), device_id_type=MESH)
    for d in range(1, 8):
        pl.semaphore_signal(barrier, inc=1, device_id=at_z((z + d) % 8), device_id_type=MESH)

    def copy(src, dst, send, recv, to):
        return pltpu.make_async_remote_copy(
            src_ref=src, dst_ref=dst, send_sem=ssem.at[send], recv_sem=rsem.at[recv],
            device_id=to, device_id_type=MESH,
        )

    def rows(start, count, step=None):
        return pl.ds(pl.multiple_of(start, step or count), count)

    def dot(a, b):
        return jnp.dot(a, b, preferred_element_type=F32)

    def dot_t(a, b):
        return lax.dot_general(a, b, (((0,), (0,)), ((), ())), preferred_element_type=F32)

    def dot_nt(a, b):
        return lax.dot_general(a, b, (((1,), (1,)), ((), ())), preferred_element_type=F32)

    def split(value):
        high = value.astype(BF16)
        return high, (value - high.astype(F32)).astype(BF16)

    row_id = lax.broadcasted_iota(jnp.int32, (16, K), 0)

    def row_of(tile):
        return jnp.concatenate([tile[i : i + 1, :] for i in range(4)], 1)

    def ratio_e():
        approx = dot(debf[0:16, :], abf[...])
        return mag[1024:1025, :] / approx[0:1, :]

    def set_row(row):
        drow[...] = row
        high, low = split(jnp.where(row_id == 0, row, 0.0))
        debf[0:16, :] = high
        debf[16:32, :] = low

    def products(high, low, ratio):
        rh, rl = split(ratio)
        left = jnp.concatenate([high, high, low], 0)
        update = dot_t(left, jnp.concatenate([rh, rl, rh], 0))
        count = high.shape[0]
        return update, dot_t(left[count:], jnp.ones((2 * count, 128), BF16))

    def first_half(high, low, target):
        ratio = target / dot(high, abf[...])
        update, total = products(high, low, ratio)
        upd[...] += update
        csum[...] += total

    def start_first_half():
        ratio = jnp.where(row_id == 0, ratio_e(), 0.0)
        update, total = products(debf[0:16, :], debf[16:32, :], ratio)
        upd[...] = update
        csum[...] = total

    def set_act():
        value = a_out[...]
        abf[...] = value.astype(BF16)
        atbf[...] = value.T.astype(BF16)

    def finish_first_half():
        scale = 1.0 / csum[...]
        for i in range(4):
            cols = slice(i * 128, i * 128 + 128)
            a_out[:, cols] = a_out[:, cols] * upd[:, cols] * scale
        set_act()

    def build(c, second):
        for i in range(8):
            start = c * 1024 + second * 8 + i
            value = samples[pl.ds(start, 128, stride=8), :] * window[second * 8 + i : second * 8 + i + 1, :]
            cols = slice(second * 1024 + i * 128, second * 1024 + i * 128 + 128)
            frames[c * 128 : c * 128 + 128, cols] = value.astype(BF16)

    samples[4096:4104, :] = jnp.zeros((8, 128), F32)
    for c in range(4):
        loads[8 + c].wait()
        build(c, 0)
        if c:
            build(c - 1, 1)
    for i in (5, 6, 7, 3, 1, 0, 2):
        loads[i].start()
    build(3, 1)

    for c in range(4):
        if c == 1:
            pl.semaphore_wait(barrier, 16)
            greet = pltpu.make_async_remote_copy(
                src_ref=samples.at[0:8, :], dst_ref=halo, send_sem=hsem.at[0], recv_sem=hsem.at[1],
                device_id=before, device_id_type=MESH,
            )
            greet.start()
        part = slice(c * 512, c * 512 + 512)
        loads[4 + c].wait()
        spec[part, :] = dot_nt(tab[part, :], frames[...])
    loads[3].wait()
    spec[2048:2064, :] = dot_nt(tab[2048:2064, :], frames[...])

    for i in range(3):
        loads[i].wait()
    atom_row = lax.broadcasted_iota(jnp.int32, (8, K), 1).astype(F32)[0:1]
    atom_col = lax.broadcasted_iota(jnp.int32, (K, 128), 0).astype(F32)
    inverse = 1.0 / atom_scale(atom_row)
    scale = atom_scale(atom_col)
    for i in range(4):
        cols = slice(i * 128, i * 128 + 128)
        value = a_out[:, cols] * scale
        a_out[:, cols] = value
        abf[:, cols] = value.astype(BF16)

    set_row(drow[...] * inverse)

    greet.wait()
    keep = jnp.where(tm == 63, 0.0, 1.0)
    tail[...] = jnp.zeros((128, 1024), BF16)
    last = halo[...] * window[8:16, :] * keep
    last = jnp.concatenate([last[c : c + 1, :] for c in range(8)], 1)
    row_16 = lax.broadcasted_iota(jnp.int32, (16, 1024), 0)
    tail[112:128, :] = jnp.where(row_16 == 15, last, 0.0).astype(BF16)
    spec[:, 384:512] += dot_nt(tab[:, 1024:2048], tail[...])

    real, imag = spec[2048:2049, :], spec[2056:2057, :]
    mag[1024:1025, :] = jnp.sqrt(real * real + imag * imag + 0.01)
    start_first_half()

    @pl.loop(0, 4)
    def _(c):
        real, imag = spec[rows(c * 256, 256), :], spec[rows(1024 + c * 256, 256), :]
        target = jnp.sqrt(real * real + imag * imag + 0.01)
        mag[rows(c * 256, 256), :] = target
        value = dland[rows(c * 256, 256), :] * inverse
        dland[rows(c * 256, 256), :] = value
        high, low = split(value)
        first_half(high, low, target)

    finish_first_half()

    near = (2, 1, 3)
    near_z = (4, 3, 5, 2, 6, 1, 7)
    pairs = ((4, 3), (5, 2), (6, 1), (7, 0))

    @pl.loop(0, ITERS)
    def _(t):
        def send(*args):
            copy(*args).start()

        def arrived(dst, recv):
            copy(dst, dst, 0, recv, core).wait_recv()

        def left(src, sent):
            copy(src, src, sent, 0, core).wait_send()

        def block(half, p, i, zz):
            return half * 512 + p * 256 + i * 64 + zz * 8

        def group(half, g):
            return [
                block(half, p, i, (z + zd) % 8) for p in range(2) for i in range(4) for zd in pairs[g]
            ]

        def gather(ref, starts):
            return jnp.concatenate([ref[rows(start, 8), :] for start in starts], 0)

        def numerator(half, g):
            starts = group(half, g)
            ratio = gather(mag, starts) / dot(gather(dland, starts).astype(BF16), abf[...])
            return dot(ratio.astype(BF16), atbf[...])

        def exchange_e(sem, dst, me, at, count, order):
            for d in order:
                send(dst.at[me], dst.at[me], sem, sem, at((me + d) % count))


        def to_core(g):
            cs[g] = numerator(1 - k, g)
            send(cs.at[g], cr.at[g], CORE + g, CORE + g, core)

        def to_first(g):
            value = numerator(k, g)
            arrived(cr.at[g], CORE + g)
            own[g] = value + cr[g]
            for q in range(2):
                zz = (z + pairs[g][q]) % 8
                for d in near:
                    for p in range(2):
                        me, at = axes[p][0]
                        to = (me + d) % 4
                        send(
                            own.at[g, rows(p * 64 + to * 16 + q * 8, 8), :], r1.at[p, me, zz],
                            P1 + p, P1 + p * 8 + zz, at(to),
                        )
            for q in range(2):
                zz = (z + pairs[g][q]) % 8
                for p in range(2):
                    me = axes[p][0][0]
                    r1[p, me, zz] = own[g, rows(p * 64 + me * 16 + q * 8, 8), :]

        def to_second(zd):
            zz = (z + zd) % 8
            for p in range(2):
                me, at = axes[p][1]
                arrived(dland.at[0:24, :], P1 + p * 8 + zz)
                total = (r1[p, 0, zz] + r1[p, 1, zz]) + (r1[p, 2, zz] + r1[p, 3, zz])
                for j in range(4):
                    s2[p, zz, j] = total[:, j * 128 : j * 128 + 128]
                for d in near:
                    to = (me + d) % 4
                    send(s2.at[p, zz, to], r2.at[p, me, zz], P2 + p, P2 + p * 8 + zz, at(to))
                r2[p, me, zz] = s2[p, zz, me]

        def to_third(zd):
            zz = (z + zd) % 8
            for p in range(2):
                arrived(s3.at[p, 0:3], P2 + p * 8 + zz)
                total = (r2[p, 0, zz] + r2[p, 1, zz]) + (r2[p, 2, zz] + r2[p, 3, zz])
                if zd:
                    s3[p, zz] = total
                    send(s3.at[p, zz], r3.at[p, z], P3 + p, P3 + p, at_z(zz))
                else:
                    r3[p, z] = total

        to_core(0)
        ratio = jnp.where(row_id == 0, ratio_e(), jnp.where(row_id == 8, 1.0, 0.0)).astype(BF16)
        line = dot(ratio, atbf[...])
        es[...] = jnp.concatenate(
            [line[r : r + 1, i * 128 : i * 128 + 128] for r in (0, 8) for i in range(4)], 0
        )
        send(es, er, CORE_E, CORE_E, core)
        to_core(1)
        arrived(er, CORE_E)
        re1[x] = es[...] + er[...]
        exchange_e(E1, re1, x, at_x, 4, near)
        to_first(0)
        to_core(2)
        to_first(1)
        to_core(3)
        to_first(2)
        to_first(3)

        arrived(re1.at[0:3], E1)
        re2[y] = (re1[0] + re1[1]) + (re1[2] + re1[3])
        exchange_e(E2, re2, y, at_y, 4, near)
        for zd in (4, 3, 5, 2, 6):
            to_second(zd)
        arrived(re2.at[0:3], E2)
        re3[z] = (re2[0] + re2[1]) + (re2[2] + re2[3])
        exchange_e(E3, re3, z, at_z, 8, near_z)
        to_third(4)
        to_second(1)
        to_third(3)
        to_second(7)
        to_third(5)
        to_second(0)
        for zd in (2, 6, 1, 7, 0):
            to_third(zd)

        def tile_of(p, zz):
            (me, _), (other, _) = axes[p]
            return dland.at[rows(block(k, p, me, zz), 8), pl.ds(pl.multiple_of(other * 128, 128), 128)]

        for p in range(2):
            arrived(r3.at[p, 0:7], P3 + p)
            total = ((r3[p, 0] + r3[p, 1]) + (r3[p, 2] + r3[p, 3])) + ((r3[p, 4] + r3[p, 5]) + (r3[p, 6] + r3[p, 7]))
            if p == 0:
                arrived(re3.at[0:7], E3)
                esum[...] = ((re3[0] + re3[1]) + (re3[2] + re3[3])) + ((re3[4] + re3[5]) + (re3[6] + re3[7]))
            tile = tile_of(p, z)
            tile[...] = tile[...] * total / esum[pl.ds(4 + axes[p][1][0], 1), :]
            for d in near_z:
                send(tile, tile, G3 + p, G3 + p * 8 + z, at_z((z + d) % 8))

        def along_second(zd):
            zz = (z + zd) % 8
            for p in range(2):
                me, at = axes[p][1]
                tile = tile_of(p, zz)
                if zd:
                    arrived(tile, G3 + p * 8 + zz)
                for d in near:
                    send(tile, tile, G2 + p, G2 + p * 8 + zz, at((me + d) % 4))

        def along_first(zd):
            zz = (z + zd) % 8
            for p in range(2):
                me, at = axes[p][0]
                arrived(dland.at[0:24, 0:128], G2 + p * 8 + zz)
                piece = dland.at[rows(block(k, p, me, zz), 8), :]
                for d in near:
                    send(piece, piece, G1 + p, G1 + p * 8 + zz, at((me + d) % 4))
                send(piece, piece, GC + p, GC + p * 8 + zz, core)

        along_second(0)
        esum_v = esum[...]
        set_row(drow[...] * row_of(esum_v[0:4, :]) / row_of(esum_v[4:8, :]))

        for zd in (1, 7, 2, 6):
            along_second(zd)
        along_first(0)
        for zd in (3, 5, 4):
            along_second(zd)
        for zd in (1, 7, 2, 6, 3, 5, 4):
            along_first(zd)

        def consume(half, g):
            @pl.when(t < ITERS - 1)
            def _():
                starts = group(half, g)
                high, low = split(gather(dland, starts))
                first_half(high, low, gather(mag, starts))

        def across(*distances):
            for zd in distances:
                zz = (z + zd) % 8
                for p in range(2):
                    me = axes[p][0][0]
                    arrived(dland.at[0:24, :], G1 + p * 8 + zz)
                    for d in (1, 3, 2):
                        piece = dland.at[rows(block(k, p, (me + d) % 4, zz), 8), :]
                        send(piece, piece, GC + p, GC + p * 8 + zz, core)

        def from_core(g):
            for zd in pairs[g]:
                zz = (z + zd) % 8
                for p in range(2):
                    arrived(dland.at[0:32, :], GC + p * 8 + zz)
            consume(1 - k, g)

        @pl.when(t < ITERS - 1)
        def _():
            start_first_half()

        across(0, 1, 7)
        consume(k, 3)
        across(2, 6)
        consume(k, 2)
        from_core(3)
        across(3, 5)
        consume(k, 1)
        from_core(2)
        across(4)

        @pl.when(t == ITERS - 1)
        def _():
            stores[1].start()

        consume(k, 0)
        from_core(1)
        from_core(0)

        @pl.when(t < ITERS - 1)
        def _():
            finish_first_half()

        @pl.when(t == ITERS - 2)
        def _():
            stores[0].start()

        left(es, CORE_E)
        for g in range(4):
            left(cs.at[g], CORE + g)
        for p in range(2):
            left(dland.at[0:192, :], P1 + p)
            left(dland.at[0:192, 0:128], P2 + p)
            left(s3.at[p, 0:7], P3 + p)
            left(s3.at[p, 0:7], G3 + p)
            left(dland.at[0:192, 0:128], G2 + p)
            left(dland.at[0:192, :], G1 + p)
            left(dland.at[0:256, :], GC + p)
        left(re1.at[0:3], E1)
        left(re2.at[0:3], E2)
        left(re3.at[0:7], E3)

    stores[2].start()
    stores[3].start()
    for copied in stores:
        copied.wait()


def nmf(wave, dictionary, activations):
    vmem = pl.BlockSpec(memory_space=pltpu.VMEM)
    hbm = pl.BlockSpec(memory_space=pltpu.HBM)
    return pl.pallas_call(
        nmf_kernel,
        out_shape=[
            jax.ShapeDtypeStruct((BINS, K), F32),
            jax.ShapeDtypeStruct((K, 512), F32),
        ],
        in_specs=[hbm, hbm, vmem, hbm, hbm],
        out_specs=[hbm] * 2,
        scratch_shapes=[
            pltpu.VMEM((K, 512), F32),
            pltpu.VMEM((4104, 128), F32),
            pltpu.VMEM((512, WIN), BF16),
            pltpu.VMEM((8, 128), F32),
            pltpu.VMEM((128, HOP), BF16),
            pltpu.VMEM((2064, WIN), BF16),
            pltpu.VMEM((2064, 512), F32),
            pltpu.VMEM((1025, 512), F32),
            pltpu.VMEM((1024, K), F32),
            pltpu.VMEM((32, K), BF16),
            pltpu.VMEM((1, K), F32),
            pltpu.VMEM((K, 512), BF16),
            pltpu.VMEM((512, K), BF16),
            pltpu.VMEM((K, 512), F32),
            pltpu.VMEM((K, 128), F32),
            pltpu.VMEM((4, 128, K), F32),
            pltpu.VMEM((4, 128, K), F32),
            pltpu.VMEM((8, 128), F32),
            pltpu.VMEM((8, 128), F32),
            pltpu.VMEM((4, 128, K), F32),
            pltpu.VMEM((2, 4, 8, 8, K), F32),
            pltpu.VMEM((2, 4, 8, 8, 128), F32),
            pltpu.VMEM((2, 8, 8, 128), F32),
            pltpu.VMEM((2, 8, 4, 8, 128), F32),
            pltpu.VMEM((2, 8, 8, 128), F32),
            pltpu.VMEM((4, 8, 128), F32),
            pltpu.VMEM((4, 8, 128), F32),
            pltpu.VMEM((8, 8, 128), F32),
            pltpu.VMEM((8, 128), F32),
            pltpu.SemaphoreType.DMA((SEMS,)),
            pltpu.SemaphoreType.DMA((SEMS,)),
            pltpu.SemaphoreType.DMA((16,)),
            pltpu.SemaphoreType.DMA((2,)),
        ],
        compiler_params=pltpu.CompilerParams(
            collective_id=0, has_side_effects=True, vmem_limit_bytes=58 * 2**20
        ),
        name="nmf",
    )(wave, jnp.asarray(make_table()), jnp.asarray(make_window()), dictionary, activations)


def unscale_kernel(d, a, d_result, a_result, dv, av, sem_in, sem_out):
    parts = [(d, dv, d_result, slice(c * 256, c * 256 + 256)) for c in range(4)]
    parts += [(a, av, a_result, slice(c * 256, c * 256 + 256)) for c in range(2)]
    parts += [(d, dv, d_result, slice(1024, 1025))]
    loads = [
        pltpu.make_async_copy(source.at[part, :], held.at[part, :], sem_in.at[n])
        for n, (source, held, _, part) in enumerate(parts)
    ]
    stores = [
        pltpu.make_async_copy(held.at[part, :], result.at[part, :], sem_out.at[n])
        for n, (_, held, result, part) in enumerate(parts)
    ]
    for load in loads:
        load.start()
    atom_row = atom_scale(lax.broadcasted_iota(jnp.int32, (8, K), 1).astype(F32)[0:1])
    for n, (_, held, _, part) in enumerate(parts):
        loads[n].wait()
        if held is dv:
            dv[part, :] = dv[part, :] * atom_row
        else:
            atom_col = (lax.broadcasted_iota(jnp.int32, (256, 128), 0) + part.start).astype(F32)
            inverse = 1.0 / atom_scale(atom_col)
            for i in range(4):
                cols = slice(i * 128, i * 128 + 128)
                av[part, cols] = av[part, cols] * inverse
        stores[n].start()
    for store in stores:
        store.wait()


def unscale(dictionary, activations):
    hbm = pl.BlockSpec(memory_space=pltpu.HBM)
    return pl.pallas_call(
        unscale_kernel,
        out_shape=[
            jax.ShapeDtypeStruct((BINS, K), F32),
            jax.ShapeDtypeStruct((K, 512), F32),
        ],
        in_specs=[hbm] * 2,
        out_specs=[hbm] * 2,
        scratch_shapes=[
            pltpu.VMEM((BINS, K), F32),
            pltpu.VMEM((K, 512), F32),
            pltpu.SemaphoreType.DMA((7,)),
            pltpu.SemaphoreType.DMA((7,)),
        ],
        compiler_params=pltpu.CompilerParams(vmem_limit_bytes=58 * 2**20),
        name="unscale",
    )(dictionary, activations)


def per_device(wave, dict_init, act_init):
    dictionary, activations = unscale(*nmf(wave.reshape(-1, 128), dict_init, act_init[0]))
    return (dictionary, activations[None])


def solution(mesh):
    in_specs = (P("corpus", "tm"), P(), P("corpus", None, "tm"))
    out_specs = (P(), P("corpus", None, "tm"))
    return jax.shard_map(
        per_device, mesh=mesh, in_specs=in_specs, out_specs=out_specs, check_vma=False
    )
```

```python
import functools

import jax
import jax.numpy as jnp
import numpy as np
from jax import lax
from jax.experimental import pallas as pl
from jax.experimental.pallas import tpu as pltpu
from jax.sharding import PartitionSpec as P

WIN = 2048
HOP = 1024
BINS = 1025
K = 512
ITERS = 3
MESH = pl.DeviceIdType.MESH
F32 = jnp.float32
BF16 = jnp.bfloat16


def make_table():
    index_n = np.arange(WIN, dtype=np.int64)[None, :]
    index_k = np.arange(BINS, dtype=np.int64)[:, None]
    phase = (index_k * index_n % WIN).astype(np.float64) * (2.0 * np.pi / WIN)
    last = np.zeros((16, WIN))
    last[0], last[8] = np.cos(phase[BINS - 1]), np.sin(phase[BINS - 1])
    table = np.concatenate([np.cos(phase[: BINS - 1]), np.sin(phase[: BINS - 1]), last], 0)
    return table.astype(np.float32).astype(jnp.bfloat16)


def make_window():
    index_n = np.arange(WIN, dtype=np.float64)
    return (0.5 - 0.5 * np.cos(2.0 * np.pi * index_n / WIN)).astype(np.float32).reshape(16, 128)


def device(x, y, z, k):
    return (x * 16 + (y // 2) * 8 + z, (y % 2) * 2 + k)


CORE, CORE_E, E1, E2, E3, P3 = 0, 4, 5, 6, 7, 8
P1, P2, G3, G2, G1, GC = 10, 26, 42, 58, 74, 90
SEMS = 106


def atom_scale(index):
    value = index * 0.6180339887
    return 1.0 + (value - jnp.floor(value))


def nmf_kernel(
    wave, table, window, d0, a0, d_result, a_result,
    a_out,    samples, frames, halo, tail, tab, spec, mag,
    dland, debf, drow, abf, atbf, upd, csum,
    cs, cr, es, er, own,
    r1, r2, r3, s2, s3, re1, re2, re3, esum, ssem, rsem, lsem, hsem,
):
    tm, corpus = lax.axis_index("tm"), lax.axis_index("corpus")
    x, z, k = tm // 16, tm % 8, corpus % 2
    y = ((tm // 8) % 2) * 2 + corpus // 2
    core = device(x, y, z, 1 - k)

    def at_x(i):
        return device(i, y, z, k)

    def at_y(i):
        return device(x, i, z, k)

    def at_z(i):
        return device(x, y, i, k)

    axes = (((x, at_x), (y, at_y)), ((y, at_y), (x, at_x)))

    loads = [
        pltpu.make_async_copy(d0.at[0:1024, :], dland, lsem.at[0]),
        pltpu.make_async_copy(a0, a_out, lsem.at[1]),
        pltpu.make_async_copy(d0.at[1024:1025, :], drow, lsem.at[2]),
        pltpu.make_async_copy(table.at[2048:2064, :], tab.at[2048:2064, :], lsem.at[3]),
    ]
    for c in range(4):
        part = slice(c * 512, c * 512 + 512)
        loads.append(pltpu.make_async_copy(table.at[part, :], tab.at[part, :], lsem.at[4 + c]))
    for c in range(4):
        part = slice(c * 1024, c * 1024 + 1024)
        loads.append(pltpu.make_async_copy(wave.at[part, :], samples.at[part, :], lsem.at[8 + c]))
    for i in (8, 9, 10, 11, 4):
        loads[i].start()

    def store(first):
        part = pl.ds(pl.multiple_of(first, 512), 512)
        return dland.at[part, :], d_result.at[part, :]

    stores = [
        pltpu.make_async_copy(a_out, a_result, lsem.at[12]),
        pltpu.make_async_copy(*store(k * 512), lsem.at[13]),
        pltpu.make_async_copy(*store((1 - k) * 512), lsem.at[14]),
        pltpu.make_async_copy(drow, d_result.at[1024:1025, :], lsem.at[15]),
    ]

    barrier = pltpu.get_barrier_semaphore()
    before, after = ((tm + 63) % 64, corpus), ((tm + 1) % 64, corpus)
    for neighbour in (before, after):
        pl.semaphore_signal(barrier, inc=1, device_id=neighbour, device_id_type=MESH)
    pl.semaphore_signal(barrier, inc=1, device_id=core, device_id_type=MESH)
    for d in range(1, 4):
        pl.semaphore_signal(barrier, inc=1, device_id=at_x((x + d) % 4), device_id_type=MESH)
        pl.semaphore_signal(barrier, inc=1, device_id=at_y((y + d) % 4), device_id_type=MESH)
    for d in range(1, 8):
        pl.semaphore_signal(barrier, inc=1, device_id=at_z((z + d) % 8), device_id_type=MESH)

    def copy(src, dst, send, recv, to):
        return pltpu.make_async_remote_copy(
            src_ref=src, dst_ref=dst, send_sem=ssem.at[send], recv_sem=rsem.at[recv],
            device_id=to, device_id_type=MESH,
        )

    def rows(start, count, step=None):
        return pl.ds(pl.multiple_of(start, step or count), count)

    def dot(a, b):
        return jnp.dot(a, b, preferred_element_type=F32)

    def dot_t(a, b):
        return lax.dot_general(a, b, (((0,), (0,)), ((), ())), preferred_element_type=F32)

    def dot_nt(a, b):
        return lax.dot_general(a, b, (((1,), (1,)), ((), ())), preferred_element_type=F32)

    def split(value):
        high = value.astype(BF16)
        return high, (value - high.astype(F32)).astype(BF16)

    row_id = lax.broadcasted_iota(jnp.int32, (16, K), 0)

    def row_of(tile):
        return jnp.concatenate([tile[i : i + 1, :] for i in range(4)], 1)

    def ratio_e():
        approx = dot(debf[0:16, :], abf[...])
        return mag[1024:1025, :] / approx[0:1, :]

    def set_row(row):
        drow[...] = row
        high, low = split(jnp.where(row_id == 0, row, 0.0))
        debf[0:16, :] = high
        debf[16:32, :] = low

    def products(high, low, ratio):
        rh, rl = split(ratio)
        return dot_t(jnp.concatenate([high, high, low], 0), jnp.concatenate([rh, rl, rh], 0))

    def first_half(high, low, target):
        ratio = target / dot(high, abf[...])
        upd[...] += products(high, low, ratio)
        csum[...] += jnp.sum(high.astype(F32) + low.astype(F32), 0, keepdims=True)

    def start_first_half():
        ratio = jnp.where(row_id == 0, ratio_e(), 0.0)
        upd[...] = products(debf[0:16, :], debf[16:32, :], ratio)
        csum[...] = drow[...]

    def set_act():
        value = a_out[...]
        abf[...] = value.astype(BF16)
        atbf[...] = value.T.astype(BF16)

    def finish_first_half():
        scale = jnp.broadcast_to(1.0 / csum[...], (128, K)).T
        for i in range(4):
            cols = slice(i * 128, i * 128 + 128)
            a_out[:, cols] = a_out[:, cols] * upd[:, cols] * scale
        set_act()

    def build(c, second):
        for i in range(8):
            start = c * 1024 + second * 8 + i
            value = samples[pl.ds(start, 128, stride=8), :] * window[second * 8 + i : second * 8 + i + 1, :]
            cols = slice(second * 1024 + i * 128, second * 1024 + i * 128 + 128)
            frames[c * 128 : c * 128 + 128, cols] = value.astype(BF16)

    samples[4096:4104, :] = jnp.zeros((8, 128), F32)
    for c in range(4):
        loads[8 + c].wait()
        build(c, 0)
        if c:
            build(c - 1, 1)
    for i in (5, 6, 7, 3, 1, 0, 2):
        loads[i].start()
    build(3, 1)

    for c, (first, last, needed) in enumerate(((0, 512, (4,)), (512, 2064, (5, 6, 7, 3)))):
        if c == 1:
            pl.semaphore_wait(barrier, 16)
            greet = pltpu.make_async_remote_copy(
                src_ref=samples.at[0:8, :], dst_ref=halo, send_sem=hsem.at[0], recv_sem=hsem.at[1],
                device_id=before, device_id_type=MESH,
            )
            greet.start()
        for i in needed:
            loads[i].wait()
        spec[first:last, :] = dot_nt(tab[first:last, :], frames[...])

    for i in range(3):
        loads[i].wait()
    atom_row = lax.broadcasted_iota(jnp.int32, (8, K), 1).astype(F32)[0:1]
    atom_col = lax.broadcasted_iota(jnp.int32, (K, 128), 0).astype(F32)
    inverse = 1.0 / atom_scale(atom_row)
    scale = atom_scale(atom_col)
    for i in range(4):
        cols = slice(i * 128, i * 128 + 128)
        value = a_out[:, cols] * scale
        a_out[:, cols] = value
        abf[:, cols] = value.astype(BF16)

    set_row(drow[...] * inverse)

    greet.wait()
    keep = jnp.where(tm == 63, 0.0, 1.0)
    tail[...] = jnp.zeros((128, 1024), BF16)
    last = halo[...] * window[8:16, :] * keep
    last = jnp.concatenate([last[c : c + 1, :] for c in range(8)], 1)
    row_16 = lax.broadcasted_iota(jnp.int32, (16, 1024), 0)
    tail[112:128, :] = jnp.where(row_16 == 15, last, 0.0).astype(BF16)
    spec[:, 384:512] += dot_nt(tab[:, 1024:2048], tail[...])

    real, imag = spec[2048:2049, :], spec[2056:2057, :]
    mag[1024:1025, :] = jnp.sqrt(real * real + imag * imag + 0.01)
    start_first_half()

    for c in range(4):
        real, imag = spec[rows(c * 256, 256), :], spec[rows(1024 + c * 256, 256), :]
        target = jnp.sqrt(real * real + imag * imag + 0.01)
        mag[rows(c * 256, 256), :] = target
        value = dland[rows(c * 256, 256), :] * inverse
        dland[rows(c * 256, 256), :] = value
        high, low = split(value)
        first_half(high, low, target)

    finish_first_half()

    near = (2, 1, 3)
    near_z = (4, 3, 5, 2, 6, 1, 7)
    pairs = ((4, 3), (5, 2), (6, 1), (7, 0))

    @pl.loop(0, ITERS)
    def _(t):
        def send(*args):
            copy(*args).start()

        def arrived(dst, recv):
            copy(dst, dst, 0, recv, core).wait_recv()

        def left(src, sent):
            copy(src, src, sent, 0, core).wait_send()

        def block(half, p, i, zz):
            return half * 512 + p * 256 + i * 64 + zz * 8

        def group(half, g):
            return [
                block(half, p, i, (z + zd) % 8) for p in range(2) for i in range(4) for zd in pairs[g]
            ]

        def gather(ref, starts):
            return jnp.concatenate([ref[rows(start, 8), :] for start in starts], 0)

        def numerator(half, g):
            starts = group(half, g)
            ratio = gather(mag, starts) / dot(gather(dland, starts).astype(BF16), abf[...])
            return dot(ratio.astype(BF16), atbf[...])

        def exchange_e(sem, dst, me, at, count, order):
            for d in order:
                send(dst.at[me], dst.at[me], sem, sem, at((me + d) % count))


        def to_core(g):
            cs[g] = numerator(1 - k, g)
            send(cs.at[g], cr.at[g], CORE + g, CORE + g, core)

        def to_first(g):
            value = numerator(k, g)
            arrived(cr.at[g], CORE + g)
            own[g] = value + cr[g]
            for q in range(2):
                zz = (z + pairs[g][q]) % 8
                for d in near:
                    for p in range(2):
                        me, at = axes[p][0]
                        to = (me + d) % 4
                        send(
                            own.at[g, rows(p * 64 + to * 16 + q * 8, 8), :], r1.at[p, me, zz],
                            P1 + p, P1 + p * 8 + zz, at(to),
                        )
            for q in range(2):
                zz = (z + pairs[g][q]) % 8
                for p in range(2):
                    me = axes[p][0][0]
                    r1[p, me, zz] = own[g, rows(p * 64 + me * 16 + q * 8, 8), :]

        def to_second(zd):
            zz = (z + zd) % 8
            for p in range(2):
                me, at = axes[p][1]
                arrived(dland.at[0:24, :], P1 + p * 8 + zz)
                total = (r1[p, 0, zz] + r1[p, 1, zz]) + (r1[p, 2, zz] + r1[p, 3, zz])
                for j in range(4):
                    s2[p, zz, j] = total[:, j * 128 : j * 128 + 128]
                for d in near:
                    to = (me + d) % 4
                    send(s2.at[p, zz, to], r2.at[p, me, zz], P2 + p, P2 + p * 8 + zz, at(to))
                r2[p, me, zz] = s2[p, zz, me]

        def to_third(zd):
            zz = (z + zd) % 8
            for p in range(2):
                arrived(s3.at[p, 0:3], P2 + p * 8 + zz)
                total = (r2[p, 0, zz] + r2[p, 1, zz]) + (r2[p, 2, zz] + r2[p, 3, zz])
                if zd:
                    s3[p, zz] = total
                    send(s3.at[p, zz], r3.at[p, z], P3 + p, P3 + p, at_z(zz))
                else:
                    r3[p, z] = total

        to_core(0)
        ratio = jnp.where(row_id == 0, ratio_e(), jnp.where(row_id == 8, 1.0, 0.0)).astype(BF16)
        line = dot(ratio, atbf[...])
        es[...] = jnp.concatenate(
            [line[r : r + 1, i * 128 : i * 128 + 128] for r in (0, 8) for i in range(4)], 0
        )
        send(es, er, CORE_E, CORE_E, core)
        to_core(1)
        arrived(er, CORE_E)
        re1[x] = es[...] + er[...]
        exchange_e(E1, re1, x, at_x, 4, near)
        to_first(0)
        to_core(2)
        to_first(1)
        to_core(3)
        to_first(2)
        to_first(3)

        arrived(re1.at[0:3], E1)
        re2[y] = (re1[0] + re1[1]) + (re1[2] + re1[3])
        exchange_e(E2, re2, y, at_y, 4, near)
        for zd in (4, 3, 5, 2, 6):
            to_second(zd)
        arrived(re2.at[0:3], E2)
        re3[z] = (re2[0] + re2[1]) + (re2[2] + re2[3])
        exchange_e(E3, re3, z, at_z, 8, near_z)
        to_third(4)
        to_second(1)
        to_third(3)
        to_second(7)
        to_third(5)
        to_second(0)
        for zd in (2, 6, 1, 7, 0):
            to_third(zd)

        def tile_of(p, zz):
            (me, _), (other, _) = axes[p]
            return dland.at[rows(block(k, p, me, zz), 8), pl.ds(pl.multiple_of(other * 128, 128), 128)]

        for p in range(2):
            arrived(r3.at[p, 0:7], P3 + p)
            total = ((r3[p, 0] + r3[p, 1]) + (r3[p, 2] + r3[p, 3])) + ((r3[p, 4] + r3[p, 5]) + (r3[p, 6] + r3[p, 7]))
            if p == 0:
                arrived(re3.at[0:7], E3)
                esum[...] = ((re3[0] + re3[1]) + (re3[2] + re3[3])) + ((re3[4] + re3[5]) + (re3[6] + re3[7]))
            tile = tile_of(p, z)
            tile[...] = tile[...] * total / esum[pl.ds(4 + axes[p][1][0], 1), :]
            for d in near_z:
                send(tile, tile, G3 + p, G3 + p * 8 + z, at_z((z + d) % 8))

        def along_second(zd):
            zz = (z + zd) % 8
            for p in range(2):
                me, at = axes[p][1]
                tile = tile_of(p, zz)
                if zd:
                    arrived(tile, G3 + p * 8 + zz)
                for d in near:
                    send(tile, tile, G2 + p, G2 + p * 8 + zz, at((me + d) % 4))

        def along_first(zd):
            zz = (z + zd) % 8
            for p in range(2):
                me, at = axes[p][0]
                arrived(dland.at[0:24, 0:128], G2 + p * 8 + zz)
                piece = dland.at[rows(block(k, p, me, zz), 8), :]
                for d in near:
                    send(piece, piece, G1 + p, G1 + p * 8 + zz, at((me + d) % 4))
                send(piece, piece, GC + p, GC + p * 8 + zz, core)

        along_second(0)
        esum_v = esum[...]
        set_row(drow[...] * row_of(esum_v[0:4, :]) / row_of(esum_v[4:8, :]))

        for zd in (1, 7, 2, 6):
            along_second(zd)
        along_first(0)
        for zd in (3, 5, 4):
            along_second(zd)
        for zd in (1, 7, 2, 6, 3, 5, 4):
            along_first(zd)

        def consume(half, g):
            @pl.when(t < ITERS - 1)
            def _():
                starts = group(half, g)
                high, low = split(gather(dland, starts))
                first_half(high, low, gather(mag, starts))

        def across(*distances):
            for zd in distances:
                zz = (z + zd) % 8
                for p in range(2):
                    me = axes[p][0][0]
                    arrived(dland.at[0:24, :], G1 + p * 8 + zz)
                    for d in (1, 3, 2):
                        piece = dland.at[rows(block(k, p, (me + d) % 4, zz), 8), :]
                        send(piece, piece, GC + p, GC + p * 8 + zz, core)

        def from_core(g):
            for zd in pairs[g]:
                zz = (z + zd) % 8
                for p in range(2):
                    arrived(dland.at[0:32, :], GC + p * 8 + zz)
            consume(1 - k, g)

        @pl.when(t < ITERS - 1)
        def _():
            start_first_half()

        across(0, 1, 7)
        consume(k, 3)
        across(2, 6)
        consume(k, 2)
        from_core(3)
        across(3, 5)
        consume(k, 1)
        from_core(2)
        across(4)

        @pl.when(t == ITERS - 1)
        def _():
            stores[1].start()

        consume(k, 0)
        from_core(1)
        from_core(0)

        @pl.when(t < ITERS - 1)
        def _():
            finish_first_half()

        @pl.when(t == ITERS - 2)
        def _():
            stores[0].start()

        left(es, CORE_E)
        for g in range(4):
            left(cs.at[g], CORE + g)
        for p in range(2):
            left(dland.at[0:192, :], P1 + p)
            left(dland.at[0:192, 0:128], P2 + p)
            left(s3.at[p, 0:7], P3 + p)
            left(s3.at[p, 0:7], G3 + p)
            left(dland.at[0:192, 0:128], G2 + p)
            left(dland.at[0:192, :], G1 + p)
            left(dland.at[0:256, :], GC + p)
        left(re1.at[0:3], E1)
        left(re2.at[0:3], E2)
        left(re3.at[0:7], E3)

    stores[2].start()
    stores[3].start()
    for copied in stores:
        copied.wait()


def nmf(wave, dictionary, activations):
    vmem = pl.BlockSpec(memory_space=pltpu.VMEM)
    hbm = pl.BlockSpec(memory_space=pltpu.HBM)
    return pl.pallas_call(
        nmf_kernel,
        out_shape=[
            jax.ShapeDtypeStruct((BINS, K), F32),
            jax.ShapeDtypeStruct((K, 512), F32),
        ],
        in_specs=[hbm, hbm, vmem, hbm, hbm],
        out_specs=[hbm] * 2,
        scratch_shapes=[
            pltpu.VMEM((K, 512), F32),
            pltpu.VMEM((4104, 128), F32),
            pltpu.VMEM((512, WIN), BF16),
            pltpu.VMEM((8, 128), F32),
            pltpu.VMEM((128, HOP), BF16),
            pltpu.VMEM((2064, WIN), BF16),
            pltpu.VMEM((2064, 512), F32),
            pltpu.VMEM((1025, 512), F32),
            pltpu.VMEM((1024, K), F32),
            pltpu.VMEM((32, K), BF16),
            pltpu.VMEM((1, K), F32),
            pltpu.VMEM((K, 512), BF16),
            pltpu.VMEM((512, K), BF16),
            pltpu.VMEM((K, 512), F32),
            pltpu.VMEM((1, K), F32),
            pltpu.VMEM((4, 128, K), F32),
            pltpu.VMEM((4, 128, K), F32),
            pltpu.VMEM((8, 128), F32),
            pltpu.VMEM((8, 128), F32),
            pltpu.VMEM((4, 128, K), F32),
            pltpu.VMEM((2, 4, 8, 8, K), F32),
            pltpu.VMEM((2, 4, 8, 8, 128), F32),
            pltpu.VMEM((2, 8, 8, 128), F32),
            pltpu.VMEM((2, 8, 4, 8, 128), F32),
            pltpu.VMEM((2, 8, 8, 128), F32),
            pltpu.VMEM((4, 8, 128), F32),
            pltpu.VMEM((4, 8, 128), F32),
            pltpu.VMEM((8, 8, 128), F32),
            pltpu.VMEM((8, 128), F32),
            pltpu.SemaphoreType.DMA((SEMS,)),
            pltpu.SemaphoreType.DMA((SEMS,)),
            pltpu.SemaphoreType.DMA((16,)),
            pltpu.SemaphoreType.DMA((2,)),
        ],
        compiler_params=pltpu.CompilerParams(
            collective_id=0, has_side_effects=True, vmem_limit_bytes=58 * 2**20
        ),
        name="nmf",
    )(wave, jnp.asarray(make_table()), jnp.asarray(make_window()), dictionary, activations)


def unscale_kernel(d, a, d_result, a_result, dv, av, sem_in, sem_out):
    parts = [(d, dv, d_result, slice(c * 256, c * 256 + 256)) for c in range(4)]
    parts += [(a, av, a_result, slice(c * 256, c * 256 + 256)) for c in range(2)]
    parts += [(d, dv, d_result, slice(1024, 1025))]
    loads = [
        pltpu.make_async_copy(source.at[part, :], held.at[part, :], sem_in.at[n])
        for n, (source, held, _, part) in enumerate(parts)
    ]
    stores = [
        pltpu.make_async_copy(held.at[part, :], result.at[part, :], sem_out.at[n])
        for n, (_, held, result, part) in enumerate(parts)
    ]
    for load in loads:
        load.start()
    atom_row = atom_scale(lax.broadcasted_iota(jnp.int32, (8, K), 1).astype(F32)[0:1])
    for n, (_, held, _, part) in enumerate(parts):
        loads[n].wait()
        if held is dv:
            dv[part, :] = dv[part, :] * atom_row
        else:
            atom_col = (lax.broadcasted_iota(jnp.int32, (256, 128), 0) + part.start).astype(F32)
            inverse = 1.0 / atom_scale(atom_col)
            for i in range(4):
                cols = slice(i * 128, i * 128 + 128)
                av[part, cols] = av[part, cols] * inverse
        stores[n].start()
    for store in stores:
        store.wait()


def unscale(dictionary, activations):
    hbm = pl.BlockSpec(memory_space=pltpu.HBM)
    return pl.pallas_call(
        unscale_kernel,
        out_shape=[
            jax.ShapeDtypeStruct((BINS, K), F32),
            jax.ShapeDtypeStruct((K, 512), F32),
        ],
        in_specs=[hbm] * 2,
        out_specs=[hbm] * 2,
        scratch_shapes=[
            pltpu.VMEM((BINS, K), F32),
            pltpu.VMEM((K, 512), F32),
            pltpu.SemaphoreType.DMA((7,)),
            pltpu.SemaphoreType.DMA((7,)),
        ],
        compiler_params=pltpu.CompilerParams(vmem_limit_bytes=58 * 2**20),
        name="unscale",
    )(dictionary, activations)


def per_device(wave, dict_init, act_init):
    dictionary, activations = unscale(*nmf(wave.reshape(-1, 128), dict_init, act_init[0]))
    return (dictionary, activations[None])


def solution(mesh):
    in_specs = (P("corpus", "tm"), P(), P("corpus", None, "tm"))
    out_specs = (P(), P("corpus", None, "tm"))
    return jax.shard_map(
        per_device, mesh=mesh, in_specs=in_specs, out_specs=out_specs, check_vma=False
    )
```
